256 devices in a mesh: grp: 4 (over x_lo, core), col: 64 (over z, x_hi, y).
Axes of the slice: x: 4 (x_hi: 2, x_lo: 2; x = x_hi * 2 + x_lo), y: 4, z: 8, core: 2. Of those that a mesh axis runs over, the one named last changes fastest.
Arguments:
- embeddings: float32 [32768, 512], P(('grp', 'col'))
- cluster_sizes: int32 [4], P('grp'), may hold values from 2048 to 8192, as said below
Outputs:
- nearest: float32 [32768], P(('grp', 'col'))
The draws below stay inside these ranges and needn't reach their ends.
Inputs may be any that keep to these rules, and one draw needn't show every extreme that they name: `cluster_sizes`: every cluster has between a quarter of 8192 and 8192 live rows; at least one cluster is full.
All inputs are finite; a program needn't handle non-finite values.
Results may differ from the reference program's by a relative error of at most 0.00039.
Values may be sent and summed in bfloat16 or wider, within the bound.
No kernel may reach another device: no remote copies, remote signals or barrier semaphores. Data moves between devices by JAX's collectives and lax.ppermute only.
A program may use at most 64 MiB of HBM per device.

```python
import math
import jax
import jax.numpy as jnp
from jax import lax

D = 512
ROWS_DEV = 128
CAP = 8192
TOTAL = 32768
N_GRP = 4


def draw_embeddings(key, part):
    key = jax.random.fold_in(key, 11)
    key_base, key_mean, key_mix, key_scale = jax.random.split(key, 4)
    base = jax.random.normal(key_base, (TOTAL, D), jnp.float32)
    mean_scale = 1.5
    common = jax.random.normal(key_mean, (D,), jnp.float32) * mean_scale
    mixing = jnp.exp(jax.random.uniform(key_mix, (TOTAL, 1), jnp.float32, math.log(0.1), math.log(3.0)))
    offset = CAP // 2 + ROWS_DEV // 2
    partner = jnp.roll(base.reshape(N_GRP, CAP, D), -offset, axis=1).reshape(TOTAL, D)
    position = jnp.arange(TOTAL, dtype=jnp.float32)[:, None] / TOTAL
    scaling = (1.0 + 2.0 * position) * jnp.exp(jax.random.uniform(key_scale, (TOTAL, 1), jnp.float32, 0.0, math.log(4.0)))
    return ((base + mixing * partner + common) * scaling).astype(jnp.float32)


def draw_cluster_sizes(key, part):
    key = jax.random.fold_in(key, 23)
    key_sizes, key_full = jax.random.split(key)
    counts = jax.random.randint(key_sizes, (N_GRP,), CAP // 4, CAP + 1)
    full_index = jax.random.randint(key_full, (), 0, N_GRP)
    return jnp.where(jnp.arange(N_GRP) == full_index, CAP, counts).astype(jnp.int32)


def setup_inputs(seed: int = 0) -> dict:
    splits = jax.random.split(jax.random.key(seed), 3)
    embeddings = draw_embeddings(jax.random.fold_in(splits[2], 71), 0)
    cluster_sizes = draw_cluster_sizes(jax.random.fold_in(splits[2], 71), 0)
    return dict(embeddings=embeddings, cluster_sizes=cluster_sizes)


def reference(embeddings, cluster_sizes):
    row_total = embeddings.shape[0]
    centre = lax.optimization_barrier(jnp.sum(embeddings, axis=0)) / row_total
    shifted = embeddings - centre
    unit_rows = (shifted * lax.rsqrt(lax.optimization_barrier(jnp.sum(shifted * shifted, axis=1, keepdims=True)) + 1e-06)).astype(jnp.bfloat16)
    grouped = unit_rows.reshape(N_GRP, CAP, D)

    def one_cluster(inputs):
        members, live_count = inputs
        slot_ids = jnp.arange(CAP, dtype=jnp.int32)

        def one_block(block_id):
            first = (block_id * ROWS_DEV).astype(jnp.int32)
            block_rows = lax.dynamic_slice_in_dim(members, first, ROWS_DEV, 0)
            scores = jnp.dot(block_rows, members.T, preferred_element_type=jnp.float32)
            row_ids = first + jnp.arange(ROWS_DEV, dtype=jnp.int32)
            valid = (slot_ids[None, :] < live_count) & (slot_ids[None, :] != row_ids[:, None])
            best_cos = lax.optimization_barrier(jnp.max(jnp.where(valid, scores, jnp.float32(-2.0)), axis=1))
            return jnp.where(row_ids < live_count, best_cos, jnp.float32(0.0))
        return lax.map(one_block, jnp.arange(CAP // ROWS_DEV, dtype=jnp.int32)).reshape(CAP)
    nearest = lax.map(one_cluster, (grouped, cluster_sizes))
    return nearest.reshape(N_GRP * CAP)
```

```python
import functools

import jax
import jax.numpy as jnp
import numpy as np
from jax import lax
from jax.experimental import pallas as pl
from jax.experimental.pallas import tpu as pltpu
from jax.sharding import Mesh, PartitionSpec as P

AXES = ("xl", "core", "z", "xh", "y")
SIZES = (2, 2, 8, 2, 4)
NZ = 8
NQ = 8
HALF = NZ // 2
EMPTY = -2.0


def z_shift(steps):
    pairs = []
    for core in range(2):
        for z in range(NZ):
            target = (z + steps) % NZ if core == 0 else (z - steps) % NZ
            pairs.append((core * NZ + z, core * NZ + target))
    return pairs


def unit(rows, centre):
    shifted = rows - centre
    scale = lax.rsqrt(jnp.sum(shifted * shifted, axis=1, keepdims=True) + 1e-06)
    return (shifted * scale).astype(jnp.bfloat16)


def best_kernel(
    live_ref, sums_ref, own_ref, z1_ref, z2_ref, z3_ref, z4_ref, plane_ref,
    own_best, z1_best, z2_best, z3_best, z4_best, plane_best,
    far_unit, plane_unit,
):
    rows, width = own_ref.shape
    total = rows * 256
    centre = jnp.sum(sums_ref[...], axis=0) / total
    live = live_ref[0]
    core = lax.axis_index("core")
    z = lax.axis_index("z")
    q = lax.axis_index("xh") * 4 + lax.axis_index("y")
    far = (own_ref, z1_ref, z2_ref, z3_ref, z4_ref)
    for j in range(NQ):
        plane_unit[j * rows : (j + 1) * rows, :] = unit(plane_ref[j], centre)
    for k in range(HALF + 1):
        far_unit[k * rows : (k + 1) * rows, :] = unit(far[k][...], centre)
    columns = NQ * rows
    col_ids = z * columns + lax.broadcasted_iota(jnp.int32, (rows, columns), 1)
    row_iota = lax.broadcasted_iota(jnp.int32, (rows, columns), 0)
    col_best = jnp.full((1, columns), EMPTY, jnp.float32)
    outs = (own_best, z1_best, z2_best, z3_best, z4_best)
    for k in range(HALF + 1):
        zk = lax.rem(z + jnp.where(core == 0, NZ - k, k), NZ)
        row_ids = (zk * NQ + q) * rows + row_iota
        scores = lax.dot_general(
            far_unit[k * rows : (k + 1) * rows, :],
            plane_unit[...],
            (((1,), (1,)), ((), ())),
            preferred_element_type=jnp.float32,
        )
        valid = (row_ids < live) & (col_ids < live)
        if k == 0:
            valid = valid & (row_ids != col_ids)
        scores = jnp.where(valid, scores, EMPTY)
        col_best = jnp.maximum(col_best, jnp.max(scores, axis=0, keepdims=True))
        folded = scores[:, :128]
        for c in range(1, columns // 128):
            folded = jnp.maximum(folded, scores[:, c * 128 : (c + 1) * 128])
        outs[k][...] = jnp.max(folded.T, axis=0, keepdims=True)
    for j in range(NQ):
        plane_best[j, :, :] = col_best[:, j * rows : (j + 1) * rows]


def shards(embeddings, cluster_sizes):
    rows, width = embeddings.shape
    far = [
        lax.ppermute(embeddings, ("core", "z"), z_shift(k)) for k in range(1, HALF + 1)
    ]
    plane = lax.all_to_all(
        jnp.broadcast_to(embeddings, (NQ, rows, width)), ("xh", "y"), 0, 0
    )
    sums = jnp.sum(embeddings, axis=0)
    sums = lax.all_to_all(
        jnp.broadcast_to(sums, (32, 1, width)), ("xl", "core", "xh", "y"), 0, 0
    )
    sums = jnp.sum(sums, axis=0)
    sums = lax.all_to_all(jnp.broadcast_to(sums, (NZ, 1, width)), "z", 0, 0)
    line = jax.ShapeDtypeStruct((1, rows), jnp.float32)
    vmem = pl.BlockSpec(memory_space=pltpu.VMEM)
    found = pl.pallas_call(
        best_kernel,
        out_shape=(line,) * 5 + (jax.ShapeDtypeStruct((NQ, 1, rows), jnp.float32),),
        in_specs=[pl.BlockSpec(memory_space=pltpu.SMEM)] + [vmem] * 7,
        out_specs=(vmem,) * 6,
        scratch_shapes=[
            pltpu.VMEM(((HALF + 1) * rows, width), jnp.bfloat16),
            pltpu.VMEM((NQ * rows, width), jnp.bfloat16),
        ],
        compiler_params=pltpu.CompilerParams(vmem_limit_bytes=48 * 1024 * 1024),
    )(cluster_sizes, sums, embeddings, *far, plane)
    best = found[0]
    back = lax.all_to_all(found[5], ("xh", "y"), 0, 0)
    for k in range(1, HALF + 1):
        best = jnp.maximum(
            best, lax.ppermute(found[k], ("core", "z"), [(b, a) for a, b in z_shift(k)])
        )
    best = jnp.maximum(best[0], jnp.max(back[:, 0, :], axis=0))
    block = lax.axis_index("z") * NQ + lax.axis_index("xh") * 4 + lax.axis_index("y")
    row_ids = block * rows + jnp.arange(rows, dtype=jnp.int32)
    return jnp.where(row_ids < cluster_sizes[0], best, jnp.float32(0.0))


def solution(mesh):
    fine = Mesh(mesh.devices.reshape(SIZES), AXES)
    return jax.shard_map(
        shards,
        mesh=fine,
        in_specs=(P(AXES, None), P(("xl", "core"))),
        out_specs=P(AXES),
        check_vma=False,
    )
```

```python
import jax
import jax.numpy as jnp
from jax import lax
from jax.experimental import pallas as pl
from jax.experimental.pallas import tpu as pltpu
from jax.sharding import Mesh, PartitionSpec as P

AXES = ("xl", "core", "z", "xh", "y")
SIZES = (2, 2, 8, 2, 4)
NZ, NX, NY = 8, 2, 4
NQ = NX * NY
BLOCKS = NZ * NQ
HALF = NZ // 2
EMPTY = -2.0
PLANE = ((0, 0), (0, 1), (0, 3), (1, 0), (1, 1), (1, 3), (0, 2), (1, 2))


def z_shift(array, steps):
    pairs = []
    for core in range(2):
        for z in range(NZ):
            target = (z + steps) % NZ if core == 0 else (z - steps) % NZ
            pairs.append((core * NZ + z, core * NZ + target))
    return lax.ppermute(array, ("core", "z"), pairs)


def y_shift(array, steps):
    return lax.ppermute(array, "y", [(y, (y + steps) % NY) for y in range(NY)])


def x_shift(array):
    return lax.ppermute(array, "xh", [(0, 1), (1, 0)])


def head_kernel(own_ref, sums_ref):
    sums_ref[...] = jnp.broadcast_to(
        jnp.sum(own_ref[...], axis=0, keepdims=True)[None], sums_ref.shape
    )


def middle_kernel(
    sums_ref, own_ref, z1_ref, z2_ref, x1_ref, y1_ref, y3_ref,
    out_ref, zs_ref, ys_ref, xs_ref,
):
    out_ref[...] = jnp.broadcast_to(
        jnp.sum(sums_ref[...], axis=0, keepdims=True), out_ref.shape
    )
    zs_ref[0], zs_ref[1] = z1_ref[...], z2_ref[...]
    ys_ref[0], ys_ref[1] = y1_ref[...], y3_ref[...]
    xs_ref[0], xs_ref[1] = own_ref[...], x1_ref[...]


def unit(rows, centre):
    shifted = rows - centre
    scale = lax.rsqrt(jnp.sum(shifted * shifted, axis=1, keepdims=True) + 1e-06)
    return (shifted * scale).astype(jnp.bfloat16)


def best_kernel(
    live_ref, sums_ref, zs_ref, ys_ref, xs_ref, zs2_ref, ys2_ref, xs2_ref,
    back_ref, far_unit, plane_unit,
):
    own_ref = xs_ref.at[0]
    far = (own_ref, zs_ref.at[0], zs_ref.at[1], zs2_ref.at[0], zs2_ref.at[1])
    plane = (
        own_ref, ys_ref.at[0], ys_ref.at[1], xs_ref.at[1],
        ys2_ref.at[0], ys2_ref.at[1], xs2_ref.at[0], xs2_ref.at[1],
    )
    rows, width = own_ref.shape
    centre = jnp.sum(sums_ref[...], axis=0) / (rows * 4 * BLOCKS)
    live = live_ref[0]
    core, z = lax.axis_index("core"), lax.axis_index("z")
    xh, y = lax.axis_index("xh"), lax.axis_index("y")
    q = xh * NY + y
    back_ref[...] = jnp.full(back_ref.shape, EMPTY, jnp.float32)
    for j in range(NQ):
        plane_unit[j * rows : (j + 1) * rows, :] = unit(plane[j][...], centre)
    far_unit[:rows, :] = plane_unit[:rows, :]
    for k in range(1, HALF + 1):
        far_unit[k * rows : (k + 1) * rows, :] = unit(far[k][...], centre)
    plane_block = [
        z * NQ + lax.rem(xh + NX - dx, NX) * NY + lax.rem(y + NY - dy, NY)
        for dx, dy in PLANE
    ]
    far_block = [
        lax.rem(z + jnp.where(core == 0, NZ - k, k), NZ) * NQ + q
        for k in range(HALF + 1)
    ]
    lane = lax.broadcasted_iota(jnp.int32, (1, rows), 1)
    col_ids = jnp.concatenate([b * rows + lane for b in plane_block], axis=1)
    row_iota = lax.broadcasted_iota(jnp.int32, (rows, 1), 0)
    columns = NQ * rows
    col_best = jnp.full((1, columns), EMPTY, jnp.float32)
    row_best = []
    for k in range(HALF + 1):
        row_ids = far_block[k] * rows + row_iota
        scores = lax.dot_general(
            far_unit[k * rows : (k + 1) * rows, :],
            plane_unit[...],
            (((1,), (1,)), ((), ())),
            preferred_element_type=jnp.float32,
        )
        valid = (row_ids < live) & (col_ids < live)
        if k == 0:
            valid = valid & (row_ids != col_ids)
        scores = jnp.where(valid, scores, EMPTY)
        col_best = jnp.maximum(col_best, jnp.max(scores, axis=0, keepdims=True))
        folded = scores[:, :rows]
        for c in range(1, NQ):
            folded = jnp.maximum(folded, scores[:, c * rows : (c + 1) * rows])
        row_best.append(jnp.max(folded.T, axis=0, keepdims=True))
    for k in range(1, HALF + 1):
        back_ref[pl.ds(far_block[k], 1), :, :] = row_best[k][None]
    for j in range(NQ):
        best = col_best[:, j * rows : (j + 1) * rows]
        if j == 0:
            best = jnp.maximum(best, row_best[0])
        back_ref[pl.ds(plane_block[j], 1), :, :] = best[None]


def shards(embeddings, cluster_sizes):
    rows, width = embeddings.shape
    vmem = pl.BlockSpec(memory_space=pltpu.VMEM)
    small = pltpu.CompilerParams(vmem_limit_bytes=4 * 1024 * 1024)
    pair = jax.ShapeDtypeStruct((2, rows, width), jnp.float32)
    sums = pl.pallas_call(
        head_kernel,
        out_shape=jax.ShapeDtypeStruct((32, 1, width), jnp.float32),
        in_specs=[vmem],
        out_specs=vmem,
        compiler_params=small,
    )(embeddings)
    sums = lax.all_to_all(sums, ("xl", "core", "xh", "y"), 0, 0)
    z2 = z_shift(embeddings, 2)
    x1 = x_shift(embeddings)
    y1 = y_shift(embeddings, 1)
    y3 = y_shift(embeddings, 3)
    z1 = z_shift(embeddings, 1)
    sums, zs, ys, xs = pl.pallas_call(
        middle_kernel,
        out_shape=(jax.ShapeDtypeStruct((NZ, 1, width), jnp.float32), pair, pair, pair),
        in_specs=[vmem] * 7,
        out_specs=(vmem,) * 4,
        compiler_params=small,
    )(sums, embeddings, z1, z2, x1, y1, y3)
    sums = lax.all_to_all(sums, "z", 0, 0)
    zs2 = z_shift(zs, 2)
    ys2 = x_shift(ys)
    xs2 = y_shift(xs, 2)
    back = pl.pallas_call(
        best_kernel,
        out_shape=jax.ShapeDtypeStruct((BLOCKS, 1, rows), jnp.float32),
        in_specs=[pl.BlockSpec(memory_space=pltpu.SMEM)] + [vmem] * 7,
        out_specs=vmem,
        scratch_shapes=[
            pltpu.VMEM(((HALF + 1) * rows, width), jnp.bfloat16),
            pltpu.VMEM((NQ * rows, width), jnp.bfloat16),
        ],
        compiler_params=pltpu.CompilerParams(vmem_limit_bytes=20 * 1024 * 1024),
    )(cluster_sizes, sums, zs, ys, xs, zs2, ys2, xs2)
    back = lax.all_to_all(back, ("z", "xh", "y"), 0, 0)
    best = jnp.max(back[:, 0, :], axis=0)
    block = lax.axis_index("z") * NQ + lax.axis_index("xh") * NY + lax.axis_index("y")
    row_ids = block * rows + jnp.arange(rows, dtype=jnp.int32)
    return jnp.where(row_ids < cluster_sizes[0], best, jnp.float32(0.0))


def solution(mesh):
    fine = Mesh(mesh.devices.reshape(SIZES), AXES)
    return jax.shard_map(
        shards,
        mesh=fine,
        in_specs=(P(AXES, None), P(("xl", "core"))),
        out_specs=P(AXES),
        check_vma=False,
    )
```

```python
import jax
import jax.numpy as jnp
from jax import lax
from jax.experimental import pallas as pl
from jax.experimental.pallas import tpu as pltpu
from jax.sharding import Mesh, PartitionSpec as P

AXES = ("xl", "core", "z", "xh", "y")
SIZES = (2, 2, 8, 2, 4)
GRID = (8, 2, 4)
BLOCKS = 64
EMPTY = -2.0
FIRST = ((0, 0, 0), (0, 0, 2), (1, 1, 0), (5, 0, 1))
SECOND = ((0, 0, 0), (0, 0, 1), (1, 0, 0))


def minus(a, b):
    return tuple((x - y) % n for x, y, n in zip(a, b, GRID))


def tiles():
    steps = [
        tuple((x + y) % n for x, y, n in zip(f, s, GRID)) for s in SECOND for f in FIRST
    ]
    missing = {
        (z, x, y) for z in range(GRID[0]) for x in range(GRID[1]) for y in range(GRID[2])
    }
    missing.discard((0, 0, 0))
    chosen = {0: [0]}
    while missing:
        best = []
        for i, a in enumerate(steps):
            found, seen = [], set()
            for j, b in enumerate(steps):
                d = minus(b, a)
                if d in missing and d not in seen:
                    seen |= {d, minus(a, b)}
                    found.append(j)
            if len(found) > len(best):
                row, best = i, found
        for j in best:
            missing -= {minus(steps[j], steps[row]), minus(steps[row], steps[j])}
        chosen[row] = chosen.get(row, []) + best
    return steps, chosen


STEPS, TILES = tiles()


def send(array, step, sign):
    size = BLOCKS
    pairs = []
    for core in range(2):
        way = sign if core == 0 else -sign
        for i in range(size):
            at = (i // 8, i // 4 % 2, i % 4)
            z, x, y = ((a + way * s) % n for a, s, n in zip(at, step, GRID))
            pairs.append((core * size + i, core * size + z * 8 + x * 4 + y))
    return lax.ppermute(array, ("core", "z", "xh", "y"), pairs)


def head_kernel(own_ref, sums_ref):
    sums_ref[...] = jnp.broadcast_to(
        jnp.sum(own_ref[...], axis=0, keepdims=True)[None], sums_ref.shape
    )


def middle_kernel(sums_ref, *refs):
    out_ref, pack_ref = refs[-2:]
    out_ref[...] = jnp.broadcast_to(
        jnp.sum(sums_ref[...], axis=0, keepdims=True), out_ref.shape
    )
    for k, ref in enumerate(refs[:-2]):
        pack_ref[k] = ref[...]


def unit(rows, centre):
    shifted = rows - centre
    scale = lax.rsqrt(jnp.sum(shifted * shifted, axis=1, keepdims=True) + 1e-06)
    return (shifted * scale).astype(jnp.bfloat16)


def best_kernel(live_ref, sums_ref, *refs):
    n = len(SECOND)
    held, found, units = refs[:n], refs[n : 2 * n], refs[2 * n]
    rows = held[0].shape[1]
    per = len(FIRST)
    centre = jnp.sum(sums_ref[...], axis=0) / (rows * 4 * BLOCKS)
    live = live_ref[0]
    core = lax.axis_index("core")
    at = [lax.axis_index(a) for a in ("z", "xh", "y")]
    lane = lax.broadcasted_iota(jnp.int32, (1, rows), 1)
    sublane = lax.broadcasted_iota(jnp.int32, (rows, 1), 0)
    starts = []
    for k, step in enumerate(STEPS):
        units[k] = unit(held[k // per][k % per], centre)
        z, x, y = (
            lax.rem(a + jnp.where(core == 0, m - s, s), m)
            for a, s, m in zip(at, step, GRID)
        )
        starts.append((z * 8 + x * 4 + y) * rows)
    best = [None] * len(STEPS)

    def merge(k, line):
        best[k] = line if best[k] is None else jnp.maximum(best[k], line)

    for i, columns in TILES.items():
        row_ids = starts[i] + sublane
        folded = None
        for j in columns:
            scores = lax.dot_general(
                units[i],
                units[j],
                (((1,), (1,)), ((), ())),
                preferred_element_type=jnp.float32,
            )
            col_ids = starts[j] + lane
            valid = (row_ids < live) & (col_ids < live)
            if i == j:
                valid = valid & (row_ids != col_ids)
            scores = jnp.where(valid, scores, EMPTY)
            merge(j, jnp.max(scores, axis=0, keepdims=True))
            if i != j:
                folded = scores if folded is None else jnp.maximum(folded, scores)
        if folded is not None:
            merge(i, jnp.max(folded.T, axis=0, keepdims=True))
    for k in range(len(STEPS)):
        line = jnp.full((1, rows), EMPTY, jnp.float32) if best[k] is None else best[k]
        found[k // per][k % per] = line


def merge_kernel(*refs):
    n = len(SECOND)
    best = refs[0][...]
    for ref in refs[1:n]:
        best = jnp.maximum(best, ref[...])
    for k, ref in enumerate(refs[n:]):
        ref[...] = best[k]


def shards(embeddings, cluster_sizes):
    rows, width = embeddings.shape
    vmem = pl.BlockSpec(memory_space=pltpu.VMEM)
    small = pltpu.CompilerParams(vmem_limit_bytes=4 * 1024 * 1024)
    first, second = len(FIRST), len(SECOND)
    arrived = [send(embeddings, step, 1) for step in FIRST[1:]]
    sums = pl.pallas_call(
        head_kernel,
        out_shape=jax.ShapeDtypeStruct((32, 1, width), jnp.float32),
        in_specs=[vmem],
        out_specs=vmem,
        compiler_params=small,
    )(embeddings)
    sums = lax.all_to_all(sums, ("xl", "core", "xh", "y"), 0, 0)
    sums, held = pl.pallas_call(
        middle_kernel,
        out_shape=(
            jax.ShapeDtypeStruct((GRID[0], 1, width), jnp.float32),
            jax.ShapeDtypeStruct((first, rows, width), jnp.float32),
        ),
        in_specs=[vmem] * (first + 1),
        out_specs=(vmem,) * 2,
        compiler_params=small,
    )(sums, embeddings, *arrived)
    sums = lax.all_to_all(sums, "z", 0, 0)
    held = [held] + [send(held, step, 1) for step in SECOND[1:]]
    found = pl.pallas_call(
        best_kernel,
        out_shape=(jax.ShapeDtypeStruct((first, 1, rows), jnp.float32),) * second,
        in_specs=[pl.BlockSpec(memory_space=pltpu.SMEM)] + [vmem] * (second + 1),
        out_specs=(vmem,) * second,
        scratch_shapes=[pltpu.VMEM((first * second, rows, width), jnp.bfloat16)],
        compiler_params=pltpu.CompilerParams(vmem_limit_bytes=20 * 1024 * 1024),
    )(cluster_sizes, sums, *held)
    back = [send(f, step, -1) for f, step in zip(found[1:], SECOND[1:])]
    lines = pl.pallas_call(
        merge_kernel,
        out_shape=(jax.ShapeDtypeStruct((1, rows), jnp.float32),) * first,
        in_specs=[vmem] * second,
        out_specs=(vmem,) * first,
        compiler_params=small,
    )(found[0], *back)
    best = lines[0]
    for line, step in zip(lines[1:], FIRST[1:]):
        best = jnp.maximum(best, send(line, step, -1))
    block = lax.axis_index("z") * 8 + lax.axis_index("xh") * 4 + lax.axis_index("y")
    row_ids = block * rows + jnp.arange(rows, dtype=jnp.int32)
    return jnp.where(row_ids < cluster_sizes[0], best[0], jnp.float32(0.0))


def solution(mesh):
    fine = Mesh(mesh.devices.reshape(SIZES), AXES)
    return jax.shard_map(
        shards,
        mesh=fine,
        in_specs=(P(AXES, None), P(("xl", "core"))),
        out_specs=P(AXES),
        check_vma=False,
    )
```

```python
import jax
import jax.numpy as jnp
from jax import lax
from jax.experimental import pallas as pl
from jax.experimental.pallas import tpu as pltpu
from jax.sharding import Mesh, PartitionSpec as P

AXES = ("xl", "core", "z", "xh", "y")
SIZES = (2, 2, 8, 2, 4)
GRID = (8, 2, 4)
BLOCKS = 64
EMPTY = -2.0
FIRST = ((0, 0, 0), (3, 0, 0), (0, 0, 2), (7, 1, 1))
SECOND = ((0, 0, 0), (0, 0, 1), (1, 0, 0))


def minus(a, b):
    return tuple((x - y) % n for x, y, n in zip(a, b, GRID))


def tiles():
    steps = [
        tuple((x + y) % n for x, y, n in zip(f, s, GRID)) for s in SECOND for f in FIRST
    ]
    missing = {
        (z, x, y) for z in range(GRID[0]) for x in range(GRID[1]) for y in range(GRID[2])
    }
    missing.discard((0, 0, 0))
    chosen = {0: [0]}
    while missing:
        best = []
        for i, a in enumerate(steps):
            found, seen = [], set()
            for j, b in enumerate(steps):
                d = minus(b, a)
                if d in missing and d not in seen:
                    seen |= {d, minus(a, b)}
                    found.append(j)
            if len(found) > len(best):
                row, best = i, found
        for j in best:
            missing -= {minus(steps[j], steps[row]), minus(steps[row], steps[j])}
        chosen[row] = chosen.get(row, []) + best
    return steps, chosen


STEPS, TILES = tiles()


def send(array, step, sign):
    size = BLOCKS
    pairs = []
    for core in range(2):
        way = sign if core == 0 else -sign
        for i in range(size):
            at = (i // 8, i // 4 % 2, i % 4)
            z, x, y = ((a + way * s) % n for a, s, n in zip(at, step, GRID))
            pairs.append((core * size + i, core * size + z * 8 + x * 4 + y))
    return lax.ppermute(array, ("core", "z", "xh", "y"), pairs)


def head_kernel(own_ref, sums_ref):
    sums_ref[...] = jnp.broadcast_to(
        jnp.sum(own_ref[...], axis=0, keepdims=True)[None], sums_ref.shape
    )


def middle_kernel(sums_ref, *refs):
    out_ref, pack_ref = refs[-2:]
    out_ref[...] = jnp.broadcast_to(
        jnp.sum(sums_ref[...], axis=0, keepdims=True), out_ref.shape
    )
    for k, ref in enumerate(refs[:-2]):
        pack_ref[k] = ref[...]


def unit(rows, centre):
    shifted = rows - centre
    scale = lax.rsqrt(jnp.sum(shifted * shifted, axis=1, keepdims=True) + 1e-06)
    return (shifted * scale).astype(jnp.bfloat16)


def best_kernel(live_ref, sums_ref, *refs):
    n = len(SECOND)
    held, found, units = refs[:n], refs[n : 2 * n], refs[2 * n]
    rows = held[0].shape[1]
    per = len(FIRST)
    centre = jnp.sum(sums_ref[...], axis=0) / (rows * 4 * BLOCKS)
    live = live_ref[0]
    core = lax.axis_index("core")
    at = [lax.axis_index(a) for a in ("z", "xh", "y")]
    lane = lax.broadcasted_iota(jnp.int32, (1, rows), 1)
    sublane = lax.broadcasted_iota(jnp.int32, (rows, 1), 0)
    starts = []
    for k, step in enumerate(STEPS):
        units[k] = unit(held[k // per][k % per], centre)
        z, x, y = (
            lax.rem(a + jnp.where(core == 0, m - s, s), m)
            for a, s, m in zip(at, step, GRID)
        )
        starts.append((z * 8 + x * 4 + y) * rows)
    best = [None] * len(STEPS)

    def merge(k, line):
        best[k] = line if best[k] is None else jnp.maximum(best[k], line)

    for i, columns in TILES.items():
        row_ids = starts[i] + sublane
        folded = None
        for j in columns:
            scores = lax.dot_general(
                units[i],
                units[j],
                (((1,), (1,)), ((), ())),
                preferred_element_type=jnp.float32,
            )
            col_ids = starts[j] + lane
            valid = (row_ids < live) & (col_ids < live)
            if i == j:
                valid = valid & (row_ids != col_ids)
            scores = jnp.where(valid, scores, EMPTY)
            merge(j, jnp.max(scores, axis=0, keepdims=True))
            if i != j:
                folded = scores if folded is None else jnp.maximum(folded, scores)
        if folded is not None:
            merge(i, jnp.max(folded.T, axis=0, keepdims=True))
    for k in range(len(STEPS)):
        line = jnp.full((1, rows), EMPTY, jnp.float32) if best[k] is None else best[k]
        found[k // per][k % per] = line


def merge_kernel(*refs):
    n = len(SECOND)
    best = refs[0][...]
    for ref in refs[1:n]:
        best = jnp.maximum(best, ref[...])
    for k, ref in enumerate(refs[n:]):
        ref[...] = best[k]


def shards(embeddings, cluster_sizes):
    rows, width = embeddings.shape
    vmem = pl.BlockSpec(memory_space=pltpu.VMEM)
    small = pltpu.CompilerParams(vmem_limit_bytes=4 * 1024 * 1024)
    first, second = len(FIRST), len(SECOND)
    arrived = [send(embeddings, step, 1) for step in FIRST[1:]]
    sums = pl.pallas_call(
        head_kernel,
        out_shape=jax.ShapeDtypeStruct((GRID[0], 1, width), jnp.float32),
        in_specs=[vmem],
        out_specs=vmem,
        compiler_params=small,
    )(embeddings)
    sums = lax.all_to_all(sums, "z", 0, 0)
    sums, held = pl.pallas_call(
        middle_kernel,
        out_shape=(
            jax.ShapeDtypeStruct((32, 1, width), jnp.float32),
            jax.ShapeDtypeStruct((first, rows, width), jnp.float32),
        ),
        in_specs=[vmem] * (first + 1),
        out_specs=(vmem,) * 2,
        compiler_params=small,
    )(sums, embeddings, *arrived)
    sums = lax.all_to_all(sums, ("xl", "core", "xh", "y"), 0, 0)
    held = [held] + [send(held, step, 1) for step in SECOND[1:]]
    found = pl.pallas_call(
        best_kernel,
        out_shape=(jax.ShapeDtypeStruct((first, 1, rows), jnp.float32),) * second,
        in_specs=[pl.BlockSpec(memory_space=pltpu.SMEM)] + [vmem] * (second + 1),
        out_specs=(vmem,) * second,
        scratch_shapes=[pltpu.VMEM((first * second, rows, width), jnp.bfloat16)],
        compiler_params=pltpu.CompilerParams(vmem_limit_bytes=20 * 1024 * 1024),
    )(cluster_sizes, sums, *held)
    back = [send(f, step, -1) for f, step in zip(found[1:], SECOND[1:])]
    lines = pl.pallas_call(
        merge_kernel,
        out_shape=(jax.ShapeDtypeStruct((1, rows), jnp.float32),) * first,
        in_specs=[vmem] * second,
        out_specs=(vmem,) * first,
        compiler_params=small,
    )(found[0], *back)
    best = lines[0]
    for line, step in zip(lines[1:], FIRST[1:]):
        best = jnp.maximum(best, send(line, step, -1))
    block = lax.axis_index("z") * 8 + lax.axis_index("xh") * 4 + lax.axis_index("y")
    row_ids = block * rows + jnp.arange(rows, dtype=jnp.int32)
    return jnp.where(row_ids < cluster_sizes[0], best[0], jnp.float32(0.0))


def solution(mesh):
    fine = Mesh(mesh.devices.reshape(SIZES), AXES)
    return jax.shard_map(
        shards,
        mesh=fine,
        in_specs=(P(AXES, None), P(("xl", "core"))),
        out_specs=P(AXES),
        check_vma=False,
    )
```

```python
import jax
import jax.numpy as jnp
from jax import lax
from jax.experimental import pallas as pl
from jax.experimental.pallas import tpu as pltpu
from jax.sharding import Mesh, PartitionSpec as P

AXES = ("xl", "core", "z", "xh", "y")
SIZES = (2, 2, 8, 2, 4)
GRID = (8, 2, 4)
BLOCKS = 64
EMPTY = -2.0
FIRST = ((0, 0, 0), (7, 1, 0), (3, 0, 1), (0, 0, 2))
SECOND = ((0, 0, 0), (0, 0, 1), (1, 0, 0))


def minus(a, b):
    return tuple((x - y) % n for x, y, n in zip(a, b, GRID))


def tiles():
    steps = [
        tuple((x + y) % n for x, y, n in zip(f, s, GRID)) for s in SECOND for f in FIRST
    ]
    missing = {
        (z, x, y) for z in range(GRID[0]) for x in range(GRID[1]) for y in range(GRID[2])
    }
    missing.discard((0, 0, 0))
    chosen = {0: [0]}
    while missing:
        best = []
        for i, a in enumerate(steps):
            found, seen = [], set()
            for j, b in enumerate(steps):
                d = minus(b, a)
                if d in missing and d not in seen:
                    seen |= {d, minus(a, b)}
                    found.append(j)
            if len(found) > len(best):
                row, best = i, found
        for j in best:
            missing -= {minus(steps[j], steps[row]), minus(steps[row], steps[j])}
        chosen[row] = chosen.get(row, []) + best
    return steps, chosen


STEPS, TILES = tiles()


def send(array, step, sign):
    size = BLOCKS
    pairs = []
    for core in range(2):
        way = sign if core == 0 else -sign
        for i in range(size):
            at = (i // 8, i // 4 % 2, i % 4)
            z, x, y = ((a + way * s) % n for a, s, n in zip(at, step, GRID))
            pairs.append((core * size + i, core * size + z * 8 + x * 4 + y))
    return lax.ppermute(array, ("core", "z", "xh", "y"), pairs)


def head_kernel(own_ref, sums_ref):
    sums_ref[...] = jnp.broadcast_to(
        jnp.sum(own_ref[...], axis=0, keepdims=True)[None], sums_ref.shape
    )


def middle_kernel(sums_ref, *refs):
    out_ref, pack_ref = refs[-2:]
    out_ref[...] = jnp.broadcast_to(
        jnp.sum(sums_ref[...], axis=0, keepdims=True), out_ref.shape
    )
    for k, ref in enumerate(refs[:-2]):
        pack_ref[k] = ref[...]


def unit(rows, centre):
    shifted = rows - centre
    scale = lax.rsqrt(jnp.sum(shifted * shifted, axis=1, keepdims=True) + 1e-06)
    return (shifted * scale).astype(jnp.bfloat16)


def best_kernel(live_ref, sums_ref, *refs):
    n = len(SECOND)
    held, found, units = refs[:n], refs[n : 2 * n], refs[2 * n]
    rows = held[0].shape[1]
    per = len(FIRST)
    centre = jnp.sum(sums_ref[...], axis=0) / (rows * 4 * BLOCKS)
    live = live_ref[0]
    core = lax.axis_index("core")
    at = [lax.axis_index(a) for a in ("z", "xh", "y")]
    lane = lax.broadcasted_iota(jnp.int32, (1, rows), 1)
    sublane = lax.broadcasted_iota(jnp.int32, (rows, 1), 0)
    starts = []
    for k, step in enumerate(STEPS):
        units[k] = unit(held[k // per][k % per], centre)
        z, x, y = (
            lax.rem(a + jnp.where(core == 0, m - s, s), m)
            for a, s, m in zip(at, step, GRID)
        )
        starts.append((z * 8 + x * 4 + y) * rows)
    best = [None] * len(STEPS)

    def merge(k, line):
        best[k] = line if best[k] is None else jnp.maximum(best[k], line)

    for i, columns in TILES.items():
        row_ids = starts[i] + sublane
        folded = None
        for j in columns:
            scores = lax.dot_general(
                units[i],
                units[j],
                (((1,), (1,)), ((), ())),
                preferred_element_type=jnp.float32,
            )
            col_ids = starts[j] + lane
            valid = (row_ids < live) & (col_ids < live)
            if i == j:
                valid = valid & (row_ids != col_ids)
            scores = jnp.where(valid, scores, EMPTY)
            merge(j, jnp.max(scores, axis=0, keepdims=True))
            if i != j:
                folded = scores if folded is None else jnp.maximum(folded, scores)
        if folded is not None:
            merge(i, jnp.max(folded.T, axis=0, keepdims=True))
    for k in range(len(STEPS)):
        line = jnp.full((1, rows), EMPTY, jnp.float32) if best[k] is None else best[k]
        found[k // per][k % per] = line


def merge_kernel(*refs):
    n = len(SECOND)
    best = refs[0][...]
    for ref in refs[1:n]:
        best = jnp.maximum(best, ref[...])
    for k, ref in enumerate(refs[n:]):
        ref[...] = best[k]


def shards(embeddings, cluster_sizes):
    rows, width = embeddings.shape
    vmem = pl.BlockSpec(memory_space=pltpu.VMEM)
    small = pltpu.CompilerParams(vmem_limit_bytes=4 * 1024 * 1024)
    first, second = len(FIRST), len(SECOND)
    arrived = [send(embeddings, step, 1) for step in FIRST[1:]]
    sums = pl.pallas_call(
        head_kernel,
        out_shape=jax.ShapeDtypeStruct((16, 1, width), jnp.float32),
        in_specs=[vmem],
        out_specs=vmem,
        compiler_params=small,
    )(embeddings)
    sums = lax.all_to_all(sums, ("core", "z"), 0, 0)
    sums, held = pl.pallas_call(
        middle_kernel,
        out_shape=(
            jax.ShapeDtypeStruct((16, 1, width), jnp.float32),
            jax.ShapeDtypeStruct((first, rows, width), jnp.float32),
        ),
        in_specs=[vmem] * (first + 1),
        out_specs=(vmem,) * 2,
        compiler_params=small,
    )(sums, embeddings, *arrived)
    sums = lax.all_to_all(sums, ("xl", "xh", "y"), 0, 0)
    held = [held] + [send(held, step, 1) for step in SECOND[1:]]
    found = pl.pallas_call(
        best_kernel,
        out_shape=(jax.ShapeDtypeStruct((first, 1, rows), jnp.float32),) * second,
        in_specs=[pl.BlockSpec(memory_space=pltpu.SMEM)] + [vmem] * (second + 1),
        out_specs=(vmem,) * second,
        scratch_shapes=[pltpu.VMEM((first * second, rows, width), jnp.bfloat16)],
        compiler_params=pltpu.CompilerParams(vmem_limit_bytes=20 * 1024 * 1024),
    )(cluster_sizes, sums, *held)
    back = [send(f, step, -1) for f, step in zip(found[1:], SECOND[1:])]
    lines = pl.pallas_call(
        merge_kernel,
        out_shape=(jax.ShapeDtypeStruct((1, rows), jnp.float32),) * first,
        in_specs=[vmem] * second,
        out_specs=(vmem,) * first,
        compiler_params=small,
    )(found[0], *back)
    best = lines[0]
    for k in (2, 3, 1):
        best = jnp.maximum(best, send(lines[k], FIRST[k], -1))
    block = lax.axis_index("z") * 8 + lax.axis_index("xh") * 4 + lax.axis_index("y")
    row_ids = block * rows + jnp.arange(rows, dtype=jnp.int32)
    return jnp.where(row_ids < cluster_sizes[0], best[0], jnp.float32(0.0))


def solution(mesh):
    fine = Mesh(mesh.devices.reshape(SIZES), AXES)
    return jax.shard_map(
        shards,
        mesh=fine,
        in_specs=(P(AXES, None), P(("xl", "core"))),
        out_specs=P(AXES),
        check_vma=False,
    )
```

```python
import jax
import jax.numpy as jnp
from jax import lax
from jax.experimental import pallas as pl
from jax.experimental.pallas import tpu as pltpu
from jax.sharding import Mesh, PartitionSpec as P

AXES = ("xl", "core", "z", "xh", "y")
SIZES = (2, 2, 8, 2, 4)
GRID = (8, 2, 4)
BLOCKS = 64
EMPTY = -2.0
FIRST = ((0, 0, 0), (7, 1, 0), (3, 0, 1), (0, 0, 2))
SECOND = ((0, 0, 0), (0, 0, 1), (1, 0, 0))


def minus(a, b):
    return tuple((x - y) % n for x, y, n in zip(a, b, GRID))


def tiles():
    steps = [
        tuple((x + y) % n for x, y, n in zip(f, s, GRID)) for s in SECOND for f in FIRST
    ]
    missing = {
        (z, x, y) for z in range(GRID[0]) for x in range(GRID[1]) for y in range(GRID[2])
    }
    missing.discard((0, 0, 0))
    chosen = {0: [0]}
    while missing:
        best = []
        for i, a in enumerate(steps):
            found, seen = [], set()
            for j, b in enumerate(steps):
                d = minus(b, a)
                if d in missing and d not in seen:
                    seen |= {d, minus(a, b)}
                    found.append(j)
            if len(found) > len(best):
                row, best = i, found
        for j in best:
            missing -= {minus(steps[j], steps[row]), minus(steps[row], steps[j])}
        chosen[row] = chosen.get(row, []) + best
    return steps, chosen


STEPS, TILES = tiles()


def send(array, step, sign):
    size = BLOCKS
    pairs = []
    for core in range(2):
        way = sign if core == 0 else -sign
        for i in range(size):
            at = (i // 8, i // 4 % 2, i % 4)
            z, x, y = ((a + way * s) % n for a, s, n in zip(at, step, GRID))
            pairs.append((core * size + i, core * size + z * 8 + x * 4 + y))
    return lax.ppermute(array, ("core", "z", "xh", "y"), pairs)


def head_kernel(live_ref, own_ref, sums_ref, count_ref):
    count_ref[...] = jnp.full(count_ref.shape, live_ref[0], jnp.int32)
    sums_ref[...] = jnp.broadcast_to(
        jnp.sum(own_ref[...], axis=0, keepdims=True)[None], sums_ref.shape
    )


def middle_kernel(sums_ref, *refs):
    out_ref, pack_ref = refs[-2:]
    out_ref[...] = jnp.broadcast_to(
        jnp.sum(sums_ref[...], axis=0, keepdims=True), out_ref.shape
    )
    for k, ref in enumerate(refs[:-2]):
        pack_ref[k] = ref[...]


def unit(rows, centre):
    shifted = rows - centre
    scale = lax.rsqrt(jnp.sum(shifted * shifted, axis=1, keepdims=True) + 1e-06)
    return (shifted * scale).astype(jnp.bfloat16)


def best_kernel(live_ref, sums_ref, *refs):
    n = len(SECOND)
    held, found, units = refs[:n], refs[n : 2 * n], refs[2 * n]
    rows = held[0].shape[1]
    per = len(FIRST)
    centre = jnp.sum(sums_ref[...], axis=0) / (rows * 4 * BLOCKS)
    live = live_ref[...]
    core = lax.axis_index("core")
    at = [lax.axis_index(a) for a in ("z", "xh", "y")]
    lane = lax.broadcasted_iota(jnp.int32, (1, rows), 1)
    sublane = lax.broadcasted_iota(jnp.int32, (rows, 1), 0)
    starts = []
    for k, step in enumerate(STEPS):
        units[k] = unit(held[k // per][k % per], centre)
        z, x, y = (
            lax.rem(a + jnp.where(core == 0, m - s, s), m)
            for a, s, m in zip(at, step, GRID)
        )
        starts.append((z * 8 + x * 4 + y) * rows)
    best = [None] * len(STEPS)

    def merge(k, line):
        best[k] = line if best[k] is None else jnp.maximum(best[k], line)

    for i, columns in TILES.items():
        row_ids = starts[i] + sublane
        folded = None
        for j in columns:
            scores = lax.dot_general(
                units[i],
                units[j],
                (((1,), (1,)), ((), ())),
                preferred_element_type=jnp.float32,
            )
            col_ids = starts[j] + lane
            valid = (row_ids < live) & (col_ids < live)
            if i == j:
                valid = valid & (row_ids != col_ids)
            scores = jnp.where(valid, scores, EMPTY)
            merge(j, jnp.max(scores, axis=0, keepdims=True))
            if i != j:
                folded = scores if folded is None else jnp.maximum(folded, scores)
        if folded is not None:
            merge(i, jnp.max(folded.T, axis=0, keepdims=True))
    for k in range(len(STEPS)):
        line = jnp.full((1, rows), EMPTY, jnp.float32) if best[k] is None else best[k]
        found[k // per][k % per] = line


def merge_kernel(*refs):
    n = len(SECOND)
    best = refs[0][...]
    for ref in refs[1:n]:
        best = jnp.maximum(best, ref[...])
    for k, ref in enumerate(refs[n:]):
        ref[...] = best[k]


def shards(embeddings, cluster_sizes):
    rows, width = embeddings.shape
    vmem = pl.BlockSpec(memory_space=pltpu.VMEM)
    small = pltpu.CompilerParams(vmem_limit_bytes=4 * 1024 * 1024)
    first, second = len(FIRST), len(SECOND)
    arrived = [send(embeddings, step, 1) for step in FIRST[1:]]
    sums, count = pl.pallas_call(
        head_kernel,
        out_shape=(
            jax.ShapeDtypeStruct((16, 1, width), jnp.float32),
            jax.ShapeDtypeStruct((1, rows), jnp.int32),
        ),
        in_specs=[pl.BlockSpec(memory_space=pltpu.SMEM), vmem],
        out_specs=(vmem, vmem),
        compiler_params=small,
    )(cluster_sizes, embeddings)
    sums = lax.all_to_all(sums, ("core", "z"), 0, 0)
    sums, held = pl.pallas_call(
        middle_kernel,
        out_shape=(
            jax.ShapeDtypeStruct((16, 1, width), jnp.float32),
            jax.ShapeDtypeStruct((first, rows, width), jnp.float32),
        ),
        in_specs=[vmem] * (first + 1),
        out_specs=(vmem,) * 2,
        compiler_params=small,
    )(sums, embeddings, *arrived)
    sums = lax.all_to_all(sums, ("xl", "xh", "y"), 0, 0)
    held = [held] + [send(held, step, 1) for step in SECOND[1:]]
    found = pl.pallas_call(
        best_kernel,
        out_shape=(jax.ShapeDtypeStruct((first, 1, rows), jnp.float32),) * second,
        in_specs=[vmem] * (second + 2),
        out_specs=(vmem,) * second,
        scratch_shapes=[pltpu.VMEM((first * second, rows, width), jnp.bfloat16)],
        compiler_params=pltpu.CompilerParams(vmem_limit_bytes=20 * 1024 * 1024),
    )(count, sums, *held)
    back = [send(f, step, -1) for f, step in zip(found[1:], SECOND[1:])]
    lines = pl.pallas_call(
        merge_kernel,
        out_shape=(jax.ShapeDtypeStruct((1, rows), jnp.float32),) * first,
        in_specs=[vmem] * second,
        out_specs=(vmem,) * first,
        compiler_params=small,
    )(found[0], *back)
    best = lines[0]
    for k in (2, 3, 1):
        best = jnp.maximum(best, send(lines[k], FIRST[k], -1))
    block = lax.axis_index("z") * 8 + lax.axis_index("xh") * 4 + lax.axis_index("y")
    row_ids = block * rows + jnp.arange(rows, dtype=jnp.int32)
    return jnp.where(row_ids < count[0], best[0], jnp.float32(0.0))


def solution(mesh):
    fine = Mesh(mesh.devices.reshape(SIZES), AXES)
    return jax.shard_map(
        shards,
        mesh=fine,
        in_specs=(P(AXES, None), P(("xl", "core"))),
        out_specs=P(AXES),
        check_vma=False,
    )
```

```python
import jax
import jax.numpy as jnp
from jax import lax
from jax.experimental import pallas as pl
from jax.experimental.pallas import tpu as pltpu
from jax.sharding import Mesh, PartitionSpec as P

AXES = ("xl", "core", "z", "xh", "y")
SIZES = (2, 2, 8, 2, 4)
GRID = (8, 2, 4)
BLOCKS = 64
EMPTY = -2.0
FIRST = ((0, 0, 0), (7, 1, 0), (3, 0, 1), (0, 0, 2))
SECOND = ((0, 0, 0), (0, 0, 1), (1, 0, 0))


def minus(a, b):
    return tuple((x - y) % n for x, y, n in zip(a, b, GRID))


def tiles():
    steps = [
        tuple((x + y) % n for x, y, n in zip(f, s, GRID)) for s in SECOND for f in FIRST
    ]
    missing = {
        (z, x, y) for z in range(GRID[0]) for x in range(GRID[1]) for y in range(GRID[2])
    }
    missing.discard((0, 0, 0))
    chosen = {0: [0]}
    while missing:
        best = []
        for i, a in enumerate(steps):
            found, seen = [], set()
            for j, b in enumerate(steps):
                d = minus(b, a)
                if d in missing and d not in seen:
                    seen |= {d, minus(a, b)}
                    found.append(j)
            if len(found) > len(best):
                row, best = i, found
        for j in best:
            missing -= {minus(steps[j], steps[row]), minus(steps[row], steps[j])}
        chosen[row] = chosen.get(row, []) + best
    return steps, chosen


STEPS, TILES = tiles()


def send(array, step, sign):
    size = BLOCKS
    pairs = []
    for core in range(2):
        way = sign if core == 0 else -sign
        for i in range(size):
            at = (i // 8, i // 4 % 2, i % 4)
            z, x, y = ((a + way * s) % n for a, s, n in zip(at, step, GRID))
            pairs.append((core * size + i, core * size + z * 8 + x * 4 + y))
    return lax.ppermute(array, ("core", "z", "xh", "y"), pairs)


def head_kernel(own_ref, sums_ref):
    sums_ref[...] = jnp.broadcast_to(
        jnp.sum(own_ref[...], axis=0, keepdims=True)[None], sums_ref.shape
    )


def middle_kernel(sums_ref, *refs):
    out_ref, pack_ref = refs[-2:]
    out_ref[...] = jnp.broadcast_to(
        jnp.sum(sums_ref[...], axis=0, keepdims=True), out_ref.shape
    )
    for k, ref in enumerate(refs[:-2]):
        pack_ref[k] = ref[...]


def unit(rows, centre):
    shifted = rows - centre
    scale = lax.rsqrt(jnp.sum(shifted * shifted, axis=1, keepdims=True) + 1e-06)
    return (shifted * scale).astype(jnp.bfloat16)


def best_kernel(live_ref, sums_ref, *refs):
    n = len(SECOND)
    held, found, units = refs[:n], refs[n : 2 * n], refs[2 * n]
    rows = held[0].shape[1]
    per = len(FIRST)
    centre = jnp.sum(sums_ref[...], axis=0) / (rows * 4 * BLOCKS)
    live = live_ref[0]
    core = lax.axis_index("core")
    at = [lax.axis_index(a) for a in ("z", "xh", "y")]
    lane = lax.broadcasted_iota(jnp.int32, (1, rows), 1)
    sublane = lax.broadcasted_iota(jnp.int32, (rows, 1), 0)
    starts = []
    for k, step in enumerate(STEPS):
        units[k] = unit(held[k // per][k % per], centre)
        z, x, y = (
            lax.rem(a + jnp.where(core == 0, m - s, s), m)
            for a, s, m in zip(at, step, GRID)
        )
        starts.append((z * 8 + x * 4 + y) * rows)
    best = [None] * len(STEPS)

    def merge(k, line):
        best[k] = line if best[k] is None else jnp.maximum(best[k], line)

    for i, columns in TILES.items():
        row_ids = starts[i] + sublane
        folded = None
        for j in columns:
            scores = lax.dot_general(
                units[i],
                units[j],
                (((1,), (1,)), ((), ())),
                preferred_element_type=jnp.float32,
            )
            col_ids = starts[j] + lane
            valid = (row_ids < live) & (col_ids < live)
            if i == j:
                valid = valid & (row_ids != col_ids)
            scores = jnp.where(valid, scores, EMPTY)
            merge(j, jnp.max(scores, axis=0, keepdims=True))
            if i != j:
                folded = scores if folded is None else jnp.maximum(folded, scores)
        if folded is not None:
            merge(i, jnp.max(folded.T, axis=0, keepdims=True))
    for k in range(len(STEPS)):
        line = jnp.full((1, rows), EMPTY, jnp.float32) if best[k] is None else best[k]
        found[k // per][k % per] = line


def merge_kernel(*refs):
    n = len(SECOND)
    best = refs[0][...]
    for ref in refs[1:n]:
        best = jnp.maximum(best, ref[...])
    for k, ref in enumerate(refs[n:]):
        ref[...] = best[k]


def shards(embeddings, cluster_sizes):
    rows, width = embeddings.shape
    vmem = pl.BlockSpec(memory_space=pltpu.VMEM)
    small = pltpu.CompilerParams(vmem_limit_bytes=4 * 1024 * 1024)
    first, second = len(FIRST), len(SECOND)
    arrived = [send(embeddings, step, 1) for step in FIRST[1:]]
    sums = pl.pallas_call(
        head_kernel,
        out_shape=jax.ShapeDtypeStruct((16, 1, width), jnp.float32),
        in_specs=[vmem],
        out_specs=vmem,
        compiler_params=small,
    )(embeddings)
    sums = lax.all_to_all(sums, ("core", "z"), 0, 0)
    sums, held = pl.pallas_call(
        middle_kernel,
        out_shape=(
            jax.ShapeDtypeStruct((16, 1, width), jnp.float32),
            jax.ShapeDtypeStruct((first, rows, width), jnp.float32),
        ),
        in_specs=[vmem] * (first + 1),
        out_specs=(vmem,) * 2,
        compiler_params=small,
    )(sums, embeddings, *arrived)
    sums = lax.all_to_all(sums, ("xl", "xh", "y"), 0, 0)
    far = send(held, SECOND[2], 1)
    held = [held, send(held, SECOND[1], 1), far]
    found = pl.pallas_call(
        best_kernel,
        out_shape=(jax.ShapeDtypeStruct((first, 1, rows), jnp.float32),) * second,
        in_specs=[pl.BlockSpec(memory_space=pltpu.SMEM)] + [vmem] * (second + 1),
        out_specs=(vmem,) * second,
        scratch_shapes=[pltpu.VMEM((first * second, rows, width), jnp.bfloat16)],
        compiler_params=pltpu.CompilerParams(vmem_limit_bytes=20 * 1024 * 1024),
    )(cluster_sizes, sums, *held)
    back = [send(f, step, -1) for f, step in zip(found[1:], SECOND[1:])]
    lines = pl.pallas_call(
        merge_kernel,
        out_shape=(jax.ShapeDtypeStruct((1, rows), jnp.float32),) * first,
        in_specs=[vmem] * second,
        out_specs=(vmem,) * first,
        compiler_params=small,
    )(found[0], *back)
    best = lines[0]
    for k in (2, 3, 1):
        best = jnp.maximum(best, send(lines[k], FIRST[k], -1))
    block = lax.axis_index("z") * 8 + lax.axis_index("xh") * 4 + lax.axis_index("y")
    row_ids = block * rows + jnp.arange(rows, dtype=jnp.int32)
    return jnp.where(row_ids < cluster_sizes[0], best[0], jnp.float32(0.0))


def solution(mesh):
    fine = Mesh(mesh.devices.reshape(SIZES), AXES)
    return jax.shard_map(
        shards,
        mesh=fine,
        in_specs=(P(AXES, None), P(("xl", "core"))),
        out_specs=P(AXES),
        check_vma=False,
    )
```

```python
import jax
import jax.numpy as jnp
from jax import lax
from jax.experimental import pallas as pl
from jax.experimental.pallas import tpu as pltpu
from jax.sharding import Mesh, PartitionSpec as P

AXES = ("xl", "core", "z", "xh", "y")
SIZES = (2, 2, 8, 2, 4)
GRID = (8, 2, 4)
BLOCKS = 64
EMPTY = -2.0
FIRST = ((0, 0, 0), (7, 1, 0), (3, 0, 1), (0, 0, 2))
SECOND = ((0, 0, 0), (0, 0, 1), (1, 0, 0))


def minus(a, b):
    return tuple((x - y) % n for x, y, n in zip(a, b, GRID))


def tiles():
    steps = [
        tuple((x + y) % n for x, y, n in zip(f, s, GRID)) for s in SECOND for f in FIRST
    ]
    missing = {
        (z, x, y) for z in range(GRID[0]) for x in range(GRID[1]) for y in range(GRID[2])
    }
    missing.discard((0, 0, 0))
    chosen = {0: [0]}
    while missing:
        best = []
        for i, a in enumerate(steps):
            found, seen = [], set()
            for j, b in enumerate(steps):
                d = minus(b, a)
                if d in missing and d not in seen:
                    seen |= {d, minus(a, b)}
                    found.append(j)
            if len(found) > len(best):
                row, best = i, found
        for j in best:
            missing -= {minus(steps[j], steps[row]), minus(steps[row], steps[j])}
        chosen[row] = chosen.get(row, []) + best
    return steps, chosen


STEPS, TILES = tiles()


def send(array, step, sign):
    size = BLOCKS
    pairs = []
    for core in range(2):
        way = sign if core == 0 else -sign
        for i in range(size):
            at = (i // 8, i // 4 % 2, i % 4)
            z, x, y = ((a + way * s) % n for a, s, n in zip(at, step, GRID))
            pairs.append((core * size + i, core * size + z * 8 + x * 4 + y))
    return lax.ppermute(array, ("core", "z", "xh", "y"), pairs)


def head_kernel(own_ref, copy_ref, sums_ref):
    copy_ref[...] = own_ref[...]
    sums_ref[...] = jnp.broadcast_to(
        jnp.sum(own_ref[...], axis=0, keepdims=True)[None], sums_ref.shape
    )


def middle_kernel(sums_ref, *refs):
    out_ref, pack_ref = refs[-2:]
    out_ref[...] = jnp.broadcast_to(
        jnp.sum(sums_ref[...], axis=0, keepdims=True), out_ref.shape
    )
    for k, ref in enumerate(refs[:-2]):
        pack_ref[k] = ref[...]


def unit(rows, centre):
    shifted = rows - centre
    scale = lax.rsqrt(jnp.sum(shifted * shifted, axis=1, keepdims=True) + 1e-06)
    return (shifted * scale).astype(jnp.bfloat16)


def best_kernel(live_ref, sums_ref, *refs):
    n = len(SECOND)
    held, found, units = refs[:n], refs[n : 2 * n], refs[2 * n]
    rows = held[0].shape[1]
    per = len(FIRST)
    centre = jnp.sum(sums_ref[...], axis=0) / (rows * 4 * BLOCKS)
    live = live_ref[0]
    core = lax.axis_index("core")
    at = [lax.axis_index(a) for a in ("z", "xh", "y")]
    lane = lax.broadcasted_iota(jnp.int32, (1, rows), 1)
    sublane = lax.broadcasted_iota(jnp.int32, (rows, 1), 0)
    starts = []
    for k, step in enumerate(STEPS):
        units[k] = unit(held[k // per][k % per], centre)
        z, x, y = (
            lax.rem(a + jnp.where(core == 0, m - s, s), m)
            for a, s, m in zip(at, step, GRID)
        )
        starts.append((z * 8 + x * 4 + y) * rows)
    best = [None] * len(STEPS)

    def merge(k, line):
        best[k] = line if best[k] is None else jnp.maximum(best[k], line)

    for i, columns in TILES.items():
        row_ids = starts[i] + sublane
        folded = None
        for j in columns:
            scores = lax.dot_general(
                units[i],
                units[j],
                (((1,), (1,)), ((), ())),
                preferred_element_type=jnp.float32,
            )
            col_ids = starts[j] + lane
            valid = (row_ids < live) & (col_ids < live)
            if i == j:
                valid = valid & (row_ids != col_ids)
            scores = jnp.where(valid, scores, EMPTY)
            merge(j, jnp.max(scores, axis=0, keepdims=True))
            if i != j:
                folded = scores if folded is None else jnp.maximum(folded, scores)
        if folded is not None:
            merge(i, jnp.max(folded.T, axis=0, keepdims=True))
    for k in range(len(STEPS)):
        line = jnp.full((1, rows), EMPTY, jnp.float32) if best[k] is None else best[k]
        found[k // per][k % per] = line


def merge_kernel(*refs):
    n = len(SECOND)
    best = refs[0][...]
    for ref in refs[1:n]:
        best = jnp.maximum(best, ref[...])
    for k, ref in enumerate(refs[n:]):
        ref[...] = best[k]


def shards(embeddings, cluster_sizes):
    rows, width = embeddings.shape
    vmem = pl.BlockSpec(memory_space=pltpu.VMEM)
    small = pltpu.CompilerParams(vmem_limit_bytes=4 * 1024 * 1024)
    first, second = len(FIRST), len(SECOND)
    embeddings, sums = pl.pallas_call(
        head_kernel,
        out_shape=(
            jax.ShapeDtypeStruct((rows, width), jnp.float32),
            jax.ShapeDtypeStruct((16, 1, width), jnp.float32),
        ),
        in_specs=[vmem],
        out_specs=(vmem, vmem),
        compiler_params=small,
    )(embeddings)
    arrived = [send(embeddings, step, 1) for step in FIRST[1:]]
    sums = lax.all_to_all(sums, ("core", "z"), 0, 0)
    sums, held = pl.pallas_call(
        middle_kernel,
        out_shape=(
            jax.ShapeDtypeStruct((16, 1, width), jnp.float32),
            jax.ShapeDtypeStruct((first, rows, width), jnp.float32),
        ),
        in_specs=[vmem] * (first + 1),
        out_specs=(vmem,) * 2,
        compiler_params=small,
    )(sums, embeddings, *arrived)
    sums = lax.all_to_all(sums, ("xl", "xh", "y"), 0, 0)
    held = [held] + [send(held, step, 1) for step in SECOND[1:]]
    found = pl.pallas_call(
        best_kernel,
        out_shape=(jax.ShapeDtypeStruct((first, 1, rows), jnp.float32),) * second,
        in_specs=[pl.BlockSpec(memory_space=pltpu.SMEM)] + [vmem] * (second + 1),
        out_specs=(vmem,) * second,
        scratch_shapes=[pltpu.VMEM((first * second, rows, width), jnp.bfloat16)],
        compiler_params=pltpu.CompilerParams(vmem_limit_bytes=20 * 1024 * 1024),
    )(cluster_sizes, sums, *held)
    back = [send(f, step, -1) for f, step in zip(found[1:], SECOND[1:])]
    lines = pl.pallas_call(
        merge_kernel,
        out_shape=(jax.ShapeDtypeStruct((1, rows), jnp.float32),) * first,
        in_specs=[vmem] * second,
        out_specs=(vmem,) * first,
        compiler_params=small,
    )(found[0], *back)
    best = lines[0]
    for k in (2, 3, 1):
        best = jnp.maximum(best, send(lines[k], FIRST[k], -1))
    block = lax.axis_index("z") * 8 + lax.axis_index("xh") * 4 + lax.axis_index("y")
    row_ids = block * rows + jnp.arange(rows, dtype=jnp.int32)
    return jnp.where(row_ids < cluster_sizes[0], best[0], jnp.float32(0.0))


def solution(mesh):
    fine = Mesh(mesh.devices.reshape(SIZES), AXES)
    return jax.shard_map(
        shards,
        mesh=fine,
        in_specs=(P(AXES, None), P(("xl", "core"))),
        out_specs=P(AXES),
        check_vma=False,
    )
```
